256 devices in a mesh: seq: 64 (over z, y_lo, x), tp: 4 (over y_hi, core).
Axes of the slice: x: 4, y: 4 (y_hi: 2, y_lo: 2; y = y_hi * 2 + y_lo), z: 8, core: 2. Of those that a mesh axis runs over, the one named last changes fastest.
Arguments:
- queries: bfloat16 [16384, 4096], P('seq', 'tp'), may hold values from -6 to 6
- keys: bfloat16 [16384, 4096], P('seq', 'tp'), may hold values from -6 to 6
- values: bfloat16 [16384, 4096], P('seq', 'tp'), may hold values from -6 to 6
- filter_spectrum: float32 [2, 64, 256, 4096], P(None, 'seq', None, 'tp'), may hold values from -6 to 6
- weight: bfloat16 [4096, 4096], P('tp', 'seq'), may hold values from -0.09375 to 0.09375
- cotangent: bfloat16 [16384, 4096], P('seq', 'tp'), may hold values from -6 to 6
Outputs:
- output: bfloat16 [16384, 4096], P('seq', 'tp')
- grad_queries: bfloat16 [16384, 4096], P('seq', 'tp')
- grad_keys: bfloat16 [16384, 4096], P('seq', 'tp')
- grad_values: bfloat16 [16384, 4096], P('seq', 'tp')
- grad_filter: float32 [2, 64, 256, 4096], P(None, 'seq', None, 'tp')
The draws below stay inside these ranges and needn't reach their ends.
All inputs are finite; a program needn't handle non-finite values.
Results may differ from the reference program's by a relative error of at most 0.024.
Values may be sent and summed in bfloat16 or wider, within the bound.
A program may use at most 128 MiB of HBM per device.

```python
import math
import jax
import jax.numpy as jnp
from jax import lax

CHANNELS = 4096
FEATURES = 4096
TOK_DEV = 256
SPLITS = 64
TOKENS = 16384


def steps_of(own_key, dims, split, least, top_value):
    def one(axis_at, shards_of):
        heights = jax.random.uniform(jax.random.fold_in(jax.random.fold_in(own_key, 6), axis_at), (shards_of,), jnp.float32, least / len(split), top_value / len(split))
        return jnp.repeat(jnp.exp(heights), dims[axis_at] // shards_of).reshape((-1,) + (1,) * (len(dims) - axis_at - 1))

    factor_of = one(*split[0])
    for cut in split[1:]:
        factor_of = factor_of * one(*cut)
    return factor_of


def gaussian(own_key, shape, scale, reach, shards=(), kind=jnp.bfloat16):
    values = jax.random.normal(own_key, shape, jnp.float32) * scale
    if len(shards) > 0:
        values = steps_of(own_key, shape, shards, -0.22, 0.18) * values
    return jnp.clip(values, min=-reach, max=reach).astype(kind)


def setup_inputs(seed: int = 0) -> dict:
    streams_of = jax.random.split(jax.random.key(seed), 7)
    return {
        "queries": gaussian(streams_of[0], (TOKENS, CHANNELS), 1.0, 6.0, ((0, 64), (1, 4))),
        "keys": gaussian(streams_of[1], (TOKENS, CHANNELS), 1.0, 6.0, ((0, 64), (1, 4))),
        "values": gaussian(streams_of[2], (TOKENS, CHANNELS), 1.0, 6.0, ((0, 64), (1, 4))),
        "filter_spectrum": gaussian(streams_of[3], (2, SPLITS, TOK_DEV, CHANNELS), 1.0, 6.0, ((1, 64), (3, 4)), jnp.float32),
        "weight": gaussian(streams_of[4], (CHANNELS, FEATURES), CHANNELS ** -0.5, 0.09375, ((0, 4), (1, 64))),
        "cotangent": gaussian(streams_of[5], (TOKENS, FEATURES), 1.0, 6.0, ((0, 64), (1, 4))),
    }


def build_tables(tok_rows, splits):
    first = jnp.arange(tok_rows, dtype=jnp.int32)
    angle_a = (2.0 * math.pi / tok_rows) * ((first[:, None] * first[None, :]) % tok_rows).astype(jnp.float32)
    cos_a = jnp.cos(angle_a)
    sin_a = jnp.sin(angle_a)
    forward_a = jnp.stack([jnp.stack([cos_a, sin_a], 0), jnp.stack([-sin_a, cos_a], 0)], 0).astype(jnp.bfloat16)
    inverse_a = jnp.stack([jnp.stack([cos_a, -sin_a], 0), jnp.stack([sin_a, cos_a], 0)], 0).astype(jnp.bfloat16)
    second = jnp.arange(splits, dtype=jnp.int32)
    angle_b = (2.0 * math.pi / splits) * ((second[:, None] * second[None, :]) % splits).astype(jnp.float32)
    cos_b = jnp.cos(angle_b)
    sin_b = jnp.sin(angle_b)
    forward_b = jnp.stack([cos_b, -sin_b], 0).astype(jnp.bfloat16)
    inverse_b = jnp.stack([cos_b, -sin_b], 1).astype(jnp.bfloat16)
    return forward_b, forward_a, inverse_a, inverse_b


def rotate(real_part, imag_part, phase_angle, direction):
    cosine = jnp.cos(phase_angle)
    sine_part = direction * jnp.sin(phase_angle)
    return jnp.stack([real_part * cosine - imag_part * sine_part, imag_part * cosine + real_part * sine_part], 0)


def product(left, right):
    return jnp.stack([left[0] * right[0] - left[1] * right[1], left[0] * right[1] + left[1] * right[0]], 0)


def phases():
    length = TOK_DEV * SPLITS
    split_ids = jnp.arange(SPLITS, dtype=jnp.int32)
    pos_ids = jnp.arange(TOK_DEV, dtype=jnp.int32)
    return (2.0 * math.pi / length) * ((split_ids[:, None] * pos_ids[None, :]) % length).astype(jnp.float32)


def forward_spectrum(signal, tables):
    forward_b, forward_a, inverse_a, inverse_b = tables
    blocks = signal.reshape(SPLITS, TOK_DEV, CHANNELS).astype(jnp.float32)
    mixed_part = jnp.einsum('xjb,bac->xjac', forward_b.astype(jnp.float32), blocks, precision=lax.Precision.HIGHEST)
    turned = rotate(mixed_part[0], mixed_part[1], phases()[:, :, None], -1.0).astype(jnp.bfloat16)
    result = jnp.einsum('xyka,yjac->xjkc', forward_a.astype(jnp.float32), turned.astype(jnp.float32), precision=lax.Precision.HIGHEST)
    return result.astype(jnp.bfloat16)


def inverse_signal(spectra, tables):
    forward_b, forward_a, inverse_a, inverse_b = tables
    length = TOK_DEV * SPLITS
    mixed_part = jnp.einsum('xyak,yjkc->xjac', inverse_a.astype(jnp.float32), spectra.astype(jnp.float32), precision=lax.Precision.HIGHEST)
    turned = rotate(mixed_part[0], mixed_part[1], phases()[:, :, None], 1.0).astype(jnp.bfloat16)
    result = jnp.einsum('byj,yjac->bac', inverse_b.astype(jnp.float32), turned.astype(jnp.float32), precision=lax.Precision.HIGHEST)
    result = result * (1.0 / length)
    return result.reshape(TOKENS, CHANNELS).astype(jnp.bfloat16)


def reference(queries, keys, values, filter_spectrum, weight, cotangent):
    tables = build_tables(TOK_DEV, SPLITS)
    mixed_input = (keys.astype(jnp.float32) * values.astype(jnp.float32)).astype(jnp.bfloat16)
    input_spectrum = forward_spectrum(mixed_input, tables)
    filtered = product(input_spectrum.astype(jnp.float32), filter_spectrum).astype(jnp.bfloat16)
    convolved = inverse_signal(filtered, tables)
    gated = (queries.astype(jnp.float32) * convolved.astype(jnp.float32)).astype(jnp.bfloat16)
    output = jnp.dot(gated, weight, preferred_element_type=jnp.float32).astype(jnp.bfloat16)
    grad_gated = jnp.dot(cotangent, weight.T, preferred_element_type=jnp.float32)
    grad_queries = (grad_gated * convolved.astype(jnp.float32)).astype(jnp.bfloat16)
    grad_convolved = (grad_gated * queries.astype(jnp.float32)).astype(jnp.bfloat16)
    grad_spectrum = forward_spectrum(grad_convolved, tables).astype(jnp.float32)
    spec_float = input_spectrum.astype(jnp.float32)
    conj_input = jnp.stack([spec_float[0], -spec_float[1]], 0)
    grad_filter = product(conj_input, grad_spectrum) * (1.0 / TOKENS)
    conj_filter = jnp.stack([filter_spectrum[0], -filter_spectrum[1]], 0)
    grad_filtered = product(conj_filter, grad_spectrum).astype(jnp.bfloat16)
    grad_mixed = inverse_signal(grad_filtered, tables).astype(jnp.float32)
    grad_keys = (grad_mixed * values.astype(jnp.float32)).astype(jnp.bfloat16)
    grad_values = (grad_mixed * keys.astype(jnp.float32)).astype(jnp.bfloat16)
    return (output, grad_queries, grad_keys, grad_values, grad_filter)
```

```python
import math

import jax
import jax.numpy as jnp
import numpy as np
from jax import lax
from jax.experimental import pallas as pl
from jax.experimental.pallas import tpu as pltpu
from jax.sharding import PartitionSpec as P

MESH = pl.DeviceIdType.MESH
BF = jnp.bfloat16
F32 = jnp.float32

NZ, NY, NX = 8, 2, 4
NS = NZ * NY * NX
NR = NY * NX
TOK = 256
CH = 1024
OWN = CH // NS
FEAT = 64
LENGTH = TOK * NS
ROWS = NS * OWN


def tables():
    b = np.arange(NS)
    ang = 2.0 * np.pi / NS * (b[:, None] * b[None, :] % NS)
    wb = np.concatenate([np.cos(ang), -np.sin(ang)], 0)
    wbi = np.concatenate([np.cos(ang), -np.sin(ang)], 1)
    a = np.arange(TOK)
    ang = 2.0 * np.pi / TOK * (a[:, None] * a[None, :] % TOK)
    c, s = np.cos(ang), np.sin(ang)
    fwd = np.block([[c, -s], [s, c]])
    inv = np.block([[c, s], [-s, c]])
    ang = 2.0 * np.pi / LENGTH * (b[:, None] * a[None, :] % LENGTH)
    low = [jnp.asarray(t.astype(np.float32)).astype(BF) for t in (wb, wbi, fwd, inv)]
    return (*low, jnp.asarray(np.cos(ang).astype(np.float32)), jnp.asarray(np.sin(ang).astype(np.float32)))


def kernel(
    keys, values, queries, cot, filt, wt, wb, wbi, dfa, dia, cosr, sinr,
    out, gq, gk, gv, gf,
    kv, vv, qv, cotf, fv, wall, xs, xr, fs, fr, spec, gspec, s32, t32, cs, cr, gcs, gcr, gfs, gfr, gms, gmr,
    conv, gg, part, prec, osum, orec, stage,
    lsem, osem, a2s, a2r, zs, zr, ws, wr, ts, tr,
):
    s = lax.axis_index("seq")
    t = lax.axis_index("tp")
    z, r = s // NR, lax.rem(s, NR)
    yl, x = r // NX, lax.rem(r, NX)
    h, core = t // 2, lax.rem(t, 2)
    sib = h * 2 + (1 - core)
    far = (1 - h) * 2 + core

    def load(i, src, dst):
        return pltpu.make_async_copy(src, dst, lsem.at[i])

    loads = [
        load(0, wt, wall.at[z, r]),
        load(1, keys, kv),
        load(2, values, vv),
        load(3, cot, cotf.at[t]),
        load(4, filt, fv),
        load(5, queries, qv),
    ]
    for one in loads:
        one.start()

    barrier = pltpu.get_barrier_semaphore()

    def greet(i, carry):
        pl.semaphore_signal(barrier, inc=1, device_id={"seq": lax.rem(s + i, NS)}, device_id_type=MESH)
        return carry

    lax.fori_loop(1, NS, greet, 0)
    for i in range(1, 4):
        pl.semaphore_signal(barrier, inc=1, device_id={"tp": lax.rem(t + i, 4)}, device_id_type=MESH)

    def rows_out(val, dst, at, c):
        moved = val.T.astype(BF).reshape(8, OWN, TOK)
        if at is None:
            dst[pl.ds(8 * c, 8)] = moved
        else:
            dst[pl.ds(8 * c, 8), at] = moved

    def lanes(c):
        return pl.ds(pl.multiple_of(c * 128, 128), 128)

    def loop(n, body):
        def step(i, carry):
            body(i)
            return carry

        lax.fori_loop(0, n, step, 0)

    loads[1].wait()
    loads[2].wait()

    def mix(c):
        at = lanes(c)
        rows_out(kv[:, at].astype(F32) * vv[:, at].astype(F32), xs, None, c)

    loop(8, mix)
    loads[0].wait()
    loads[3].wait()

    pl.semaphore_wait(barrier, NS - 1 + 3)

    def remote(src, dst, ss, rs, **to):
        return pltpu.make_async_remote_copy(
            src_ref=src, dst_ref=dst, send_sem=ss, recv_sem=rs, device_id=to, device_id_type=MESH
        )

    def send_all(i, src, dst):
        def one(k, carry):
            d = lax.rem(s + k, NS)
            remote(src.at[d], dst.at[s], a2s.at[i], a2r.at[i], seq=d).start()
            return carry

        lax.fori_loop(1, NS, one, 0)
        dst[s] = src[s]

    def wait_all(i, src, dst):
        remote(src.at[pl.ds(0, NS - 1)], dst.at[pl.ds(0, NS - 1)], a2s.at[i], a2r.at[i], seq=s).wait_recv()

    def zdev(k):
        return lax.rem(z + k + NZ, NZ)

    def zcopy(k, way):
        src = wall.at[zdev(-k * way), r]
        if k == 3:
            src = wall.at[zdev(-k * way), r, pl.ds(0 if way > 0 else FEAT // 2, FEAT // 2)]
        i = 0 if way > 0 else 1
        return remote(src, src, zs.at[i, k], zr.at[i, k], seq=zdev(way) * NR + r)

    def zwait(k):
        for i, way in ((0, 1), (1, -1)):
            src = wall.at[zdev(-(k + 1) * way), r]
            if k == 3:
                src = wall.at[zdev(-(k + 1) * way), r, pl.ds(0 if way > 0 else FEAT // 2, FEAT // 2)]
            remote(src, src, zs.at[i, k], zr.at[i, k], seq=zdev(way) * NR + r).wait_recv()

    def zstart(k):
        zcopy(k, 1).start()
        zcopy(k, -1).start()

    def rx(k):
        return yl * NX + lax.rem(x + k + NX, NX)

    def rp(k):
        return (1 - yl) * NX + lax.rem(x + k + NX, NX)

    low, high = (0, 4), (4, 4)

    def rows(part_of, ri):
        return wall.at[pl.ds(part_of[0], part_of[1]), ri]

    plan = {
        0: (low, rx(0), rp(0), rp(0)),
        1: (high, rx(0), rx(-1), rx(1)),
        2: (high, rx(0), rx(1), rx(-1)),
        3: (high, rx(0), rp(0), rp(0)),
        4: (low, rx(0), rx(-1), rx(1)),
        5: (low, rx(0), rx(1), rx(-1)),
        6: (low, rp(0), rp(-1), rx(1)),
        7: (low, rp(0), rp(1), rx(-1)),
        8: ((4, 2), rx(-1), rx(-2), rx(1)),
        9: ((6, 2), rx(1), rx(2), rx(-1)),
        10: (high, rx(-1), rp(-1), rp(0)),
        11: (high, rx(1), rp(1), rp(0)),
        12: (high, rx(2), rp(2), rp(0)),
        13: ((0, 2), rx(-1), rx(-2), rx(1)),
        14: ((2, 2), rx(1), rx(2), rx(-1)),
        15: ((0, 2), rp(-1), rp(-2), rx(1)),
        16: ((2, 2), rp(1), rp(2), rx(-1)),
    }

    def wcopy(i, back=False):
        half, sent, received, to = plan[i]
        ref = rows(half, received if back else sent)
        return remote(ref, ref, ws.at[i], wr.at[i], seq=z * NR + to)

    def wstart(*which):
        for i in which:
            wcopy(i).start()

    def wwait(*which):
        for i in which:
            wcopy(i, True).wait_recv()

    def forward(src, dst):
        def widen(m):
            wide = src[pl.ds(8 * m, 8)].reshape(128, TOK).astype(F32)
            for lane in range(2):
                s32[lane, pl.ds(128 * m, 128)] = wide[:, 128 * lane : 128 * lane + 128]

        loop(8, widen)
        for c in range(OWN):
            at = pl.ds(c, NS, stride=OWN)
            taken = jnp.concatenate([s32[lane, at, :] for lane in range(2)], 1).astype(BF)
            y = jnp.dot(wb[...], taken, preferred_element_type=F32)
            re, im = y[:NS], y[NS:]
            tre = re * cosr[...] + im * sinr[...]
            tim = im * cosr[...] - re * sinr[...]
            for lane in range(2):
                t32[lane, at, :] = tre[:, 128 * lane : 128 * lane + 128]
                t32[2 + lane, at, :] = tim[:, 128 * lane : 128 * lane + 128]

        def second(m):
            at = pl.ds(128 * m, 128)
            left = jnp.concatenate([t32[lane, at] for lane in range(4)], 1).astype(BF)
            dst[at] = jnp.dot(left, dfa[...], preferred_element_type=F32).astype(BF)

        loop(8, second)

    def filter_at(m):
        at = pl.ds(8 * m, 8)
        return fr[at, 0].reshape(128, TOK).astype(F32), fr[at, 1].reshape(128, TOK).astype(F32)

    def inverse(src, conj, dst):
        def first(m):
            at = pl.ds(128 * m, 128)
            sre, sim = src[at, 0:TOK].astype(F32), src[at, TOK:].astype(F32)
            fre, fim = filter_at(m)
            if conj:
                fim = -fim
            y = jnp.concatenate([sre * fre - sim * fim, sre * fim + sim * fre], 1).astype(BF)
            o = jnp.dot(y, dia[...], preferred_element_type=F32)
            for lane in range(4):
                t32[lane, at] = o[:, 128 * lane : 128 * lane + 128]

        loop(8, first)
        for c in range(OWN):
            at = pl.ds(c, NS, stride=OWN)
            re = jnp.concatenate([t32[lane, at, :] for lane in range(2)], 1)
            im = jnp.concatenate([t32[2 + lane, at, :] for lane in range(2)], 1)
            tre = re * cosr[...] - im * sinr[...]
            tim = im * cosr[...] + re * sinr[...]
            both = jnp.concatenate([tre, tim], 0).astype(BF)
            o = jnp.dot(wbi[...], both, preferred_element_type=F32) * (1.0 / LENGTH)
            for lane in range(2):
                s32[lane, at, :] = o[:, 128 * lane : 128 * lane + 128]

        def narrow(m):
            wide = jnp.concatenate([s32[lane, pl.ds(128 * m, 128)] for lane in range(2)], 1)
            dst[pl.ds(8 * m, 8)] = wide.astype(BF).reshape(8, OWN, TOK)

        loop(8, narrow)

    def back_at(src, c):
        return src[pl.ds(8 * c, 8)].reshape(128, TOK).astype(F32).T

    zstart(0)
    cot_sib = remote(cotf.at[t], cotf.at[t], ts.at[0], tr.at[0], tp=sib)
    cot_far = remote(cotf.at[t], cotf.at[t], ts.at[1], tr.at[1], tp=far)
    cot_sib.start()
    cot_far.start()
    send_all(0, xs, xr)
    zwait(0)
    zstart(1)

    loads[4].wait()

    def turn_filter(c):
        at = lanes(c)
        for p in range(2):
            rows_out(fv[p, :, at], fs, p, c)

    loop(8, turn_filter)
    zwait(1)
    zstart(2)
    send_all(1, fs, fr)
    zwait(2)
    zstart(3)
    remote(cotf.at[far], cotf.at[far], ts.at[1], tr.at[1], tp=far).wait_recv()
    cot_fwd = remote(cotf.at[far], cotf.at[far], ts.at[2], tr.at[2], tp=sib)
    cot_fwd.start()
    zwait(3)
    wstart(0, 1, 2, 3, 4, 5)

    wait_all(0, xs, xr)
    forward(xr, spec)
    wwait(0)
    wstart(6, 7)
    wwait(1, 2)
    wstart(8, 9, 10, 11)
    wait_all(1, fs, fr)
    inverse(spec, False, cs)
    send_all(2, cs, cr)
    wwait(4, 5)
    wstart(13, 14)
    wwait(8, 9)
    wstart(12)
    wwait(6, 7)
    wstart(15, 16)

    remote(cotf.at[sib], cotf.at[sib], ts.at[0], tr.at[0], tp=sib).wait_recv()
    fars = (1 - h) * 2 + (1 - core)
    remote(cotf.at[fars], cotf.at[fars], ts.at[2], tr.at[2], tp=sib).wait_recv()

    def grad_block(blk, first):
        left = cotf[blk]

        def one(n):
            at = pl.ds(pl.multiple_of(n * 256, 256), 256)
            right = wall[2 * blk : 2 * blk + 2, :, :, at].reshape(CH, 256)
            y = jnp.dot(left, right, preferred_element_type=F32)
            if first:
                gg[:, at] = y
            else:
                gg[:, at] += y

        loop(4, one)

    wwait(13, 14, 15, 16)
    grad_block(0, True)
    grad_block(1, False)
    wwait(3, 10, 11, 12)
    grad_block(2, False)
    grad_block(3, False)
    loads[5].wait()

    def turn_grad(c):
        at = lanes(c)
        rows_out(gg[:, at] * qv[:, at].astype(F32), gcs, None, c)

    loop(8, turn_grad)
    send_all(3, gcs, gcr)

    wait_all(2, cs, cr)

    def gate(c):
        at = lanes(c)
        y = back_at(cr, c).astype(BF)
        yf = y.astype(F32)
        stage[0, :, at] = (gg[:, at] * yf).astype(BF)
        conv[:, at] = (qv[:, at].astype(F32) * yf).astype(BF)

    loop(8, gate)
    gq_out = pltpu.make_async_copy(stage.at[0], gq, osem.at[0])
    gq_out.start()

    def out_block(blk):
        def one(n):
            right = wall[2 * blk + n // 2, pl.ds(lax.rem(n, 2) * 4, 4)].reshape(256, CH)
            at = pl.ds(pl.multiple_of(n * 256, 256), 256)
            part[blk, :, at] = lax.dot_general(
                conv[...], right, (((1,), (1,)), ((), ())), preferred_element_type=F32
            ).astype(BF)

        loop(4, one)

    psend = []
    for k, hh in ((0, 1 - h), (1, h)):
        out_block(hh * 2 + (1 - core))
        copy = remote(part.at[hh * 2 + (1 - core)], prec.at[hh], ts.at[3 + k], tr.at[3 + k], tp=sib)
        copy.start()
        psend.append(copy)
    out_block((1 - h) * 2 + core)
    out_block(h * 2 + core)
    remote(part.at[sib], prec.at[1 - h], ts.at[3], tr.at[3], tp=sib).wait_recv()
    osum[...] = (part[(1 - h) * 2 + core].astype(F32) + prec[1 - h].astype(F32)).astype(BF)
    osend = remote(osum, orec, ts.at[5], tr.at[5], tp=far)
    osend.start()

    wait_all(3, gcs, gcr)
    forward(gcr, gspec)

    def grad_filter(m):
        at = pl.ds(128 * m, 128)
        xre, xim = spec[at, 0:TOK].astype(F32), spec[at, TOK:].astype(F32)
        gre, gim = gspec[at, 0:TOK].astype(F32), gspec[at, TOK:].astype(F32)
        scale = 1.0 / LENGTH
        gfs[pl.ds(8 * m, 8), 0] = ((xre * gre + xim * gim) * scale).astype(BF).reshape(8, OWN, TOK)
        gfs[pl.ds(8 * m, 8), 1] = ((xre * gim - xim * gre) * scale).astype(BF).reshape(8, OWN, TOK)

    loop(8, grad_filter)
    send_all(4, gfs, gfr)
    inverse(gspec, True, gms)
    send_all(5, gms, gmr)

    remote(part.at[fars], prec.at[h], ts.at[4], tr.at[4], tp=sib).wait_recv()
    osend.wait_recv()
    stage[1] = (part[t].astype(F32) + prec[h].astype(F32) + orec[...].astype(F32)).astype(BF)
    out_out = pltpu.make_async_copy(stage.at[1], out, osem.at[1])
    out_out.start()

    wait_all(4, gfs, gfr)

    def filter_back(c):
        at = lanes(c)
        for p in range(2):
            fv[p, :, at] = gfr[pl.ds(8 * c, 8), p].reshape(128, TOK).astype(F32).T

    loop(8, filter_back)
    gf_out = pltpu.make_async_copy(fv, gf, osem.at[2])
    gf_out.start()
    wait_all(5, gms, gmr)

    def finish(c):
        at = lanes(c)
        y = back_at(gmr, c)
        stage[2, :, at] = (y * vv[:, at].astype(F32)).astype(BF)
        stage[3, :, at] = (y * kv[:, at].astype(F32)).astype(BF)

    loop(8, finish)
    gk_out = pltpu.make_async_copy(stage.at[2], gk, osem.at[3])
    gv_out = pltpu.make_async_copy(stage.at[3], gv, osem.at[4])
    gk_out.start()
    gv_out.start()

    for i, src, dst in ((0, xs, xr), (1, fs, fr), (2, cs, cr), (3, gcs, gcr), (4, gfs, gfr), (5, gms, gmr)):
        remote(src.at[pl.ds(0, NS - 1)], dst.at[pl.ds(0, NS - 1)], a2s.at[i], a2r.at[i], seq=s).wait_send()
    for k in range(4):
        zcopy(k, 1).wait_send()
        zcopy(k, -1).wait_send()
    for i in plan:
        wcopy(i).wait_send()
    for copy in (cot_sib, cot_far, cot_fwd, *psend, osend):
        copy.wait_send()
    for copy in (gq_out, out_out, gf_out, gk_out, gv_out):
        copy.wait()


def shards(queries, keys, values, filter_spectrum, weight, cotangent):
    wt = weight.T
    filt = filter_spectrum.reshape(2, TOK, CH)
    anywhere = pl.BlockSpec(memory_space=pl.ANY)
    vmem = pl.BlockSpec(memory_space=pltpu.VMEM)
    flat = jax.ShapeDtypeStruct((TOK, CH), BF)
    blocks = pltpu.VMEM((NS, OWN, TOK), BF)
    pairs = pltpu.VMEM((NS, 2, OWN, TOK), BF)
    whole = pltpu.VMEM((TOK, CH), BF)
    dma = pltpu.SemaphoreType.DMA
    out, gq, gk, gv, gf = pl.pallas_call(
        kernel,
        out_shape=(flat, flat, flat, flat, jax.ShapeDtypeStruct((2, TOK, CH), F32)),
        in_specs=[anywhere] * 6 + [vmem] * 6,
        out_specs=(anywhere,) * 5,
        scratch_shapes=[
            whole, whole, whole,
            pltpu.VMEM((4, TOK, CH), BF),
            pltpu.VMEM((2, TOK, CH), F32),
            pltpu.VMEM((NZ, NR, FEAT, CH), BF),
            blocks, blocks, pairs, pairs,
            pltpu.VMEM((ROWS, 2 * TOK), BF),
            pltpu.VMEM((ROWS, 2 * TOK), BF),
            pltpu.VMEM((2, ROWS, 128), F32),
            pltpu.VMEM((4, ROWS, 128), F32),
            blocks, blocks, blocks, blocks,
            pairs, pairs, blocks, blocks,
            whole,
            pltpu.VMEM((TOK, CH), F32),
            pltpu.VMEM((4, TOK, CH), BF),
            pltpu.VMEM((2, TOK, CH), BF),
            whole, whole,
            pltpu.VMEM((4, TOK, CH), BF),
            dma((6,)), dma((5,)), dma((6,)), dma((6,)),
            dma((2, 4)), dma((2, 4)), dma((17,)), dma((17,)), dma((6,)), dma((6,)),
        ],
        compiler_params=pltpu.CompilerParams(
            collective_id=0, has_side_effects=True, vmem_limit_bytes=56 * 1024 * 1024
        ),
    )(keys, values, queries, cotangent, filt, wt, *tables())
    return out, gq, gk, gv, gf.reshape(2, 1, TOK, CH)


def solution(mesh):
    io = P("seq", "tp")
    spectrum = P(None, "seq", None, "tp")
    return jax.shard_map(
        shards,
        mesh=mesh,
        in_specs=(io, io, io, spectrum, P("tp", "seq"), io),
        out_specs=(io, io, io, io, spectrum),
        check_vma=False,
    )
```

```python
import math

import jax
import jax.numpy as jnp
import numpy as np
from jax import lax
from jax.experimental import pallas as pl
from jax.experimental.pallas import tpu as pltpu
from jax.sharding import PartitionSpec as P

MESH = pl.DeviceIdType.MESH
BF = jnp.bfloat16
F32 = jnp.float32

NZ, NY, NX = 8, 2, 4
NS = NZ * NY * NX
NR = NY * NX
TOK = 256
CH = 1024
OWN = CH // NS
FEAT = 64
LENGTH = TOK * NS
ROWS = NS * OWN


def tables():
    b = np.arange(NS)
    ang = 2.0 * np.pi / NS * (b[:, None] * b[None, :] % NS)
    wb = np.concatenate([np.cos(ang), -np.sin(ang)], 0)
    wbi = np.concatenate([np.cos(ang), -np.sin(ang)], 1)
    a = np.arange(TOK)
    ang = 2.0 * np.pi / TOK * (a[:, None] * a[None, :] % TOK)
    c, s = np.cos(ang), np.sin(ang)
    fwd = np.block([[c, -s], [s, c]])
    inv = np.block([[c, s], [-s, c]])
    ang = 2.0 * np.pi / LENGTH * (b[:, None] * a[None, :] % LENGTH)
    low = [jnp.asarray(t.astype(np.float32)).astype(BF) for t in (wb, wbi, fwd, inv)]
    return (*low, jnp.asarray(np.cos(ang).astype(np.float32)), jnp.asarray(np.sin(ang).astype(np.float32)))


def kernel(
    keys, values, queries, cot, filt, wt, wb, wbi, dfa, dia, cosr, sinr,
    out, gq, gfr, gmr,
    kv, vv, qv, cotg, cots, fv, wall, xs, xr, fs, fr, spec, gspec, s32, t32, cs, cr, gcs, gcr, gfs, gms,
    gat, gg, gsend, grecv, part, prec, ssum, orec, stage,
    lsem, osem, a2s, a2r, a2l, zs, zr, ws, wr, wfs, wfr, ts, tr, gs, gr, ps, pr,
):
    s = lax.axis_index("seq")
    t = lax.axis_index("tp")
    z, r = s // NR, lax.rem(s, NR)
    yl, x = r // NX, lax.rem(r, NX)
    h, core = t // 2, lax.rem(t, 2)
    sib = h * 2 + (1 - core)
    far = (1 - h) * 2 + core
    fars = (1 - h) * 2 + (1 - core)
    beside = z * NR + (1 - yl) * NX + x

    def load(i, src, dst):
        return pltpu.make_async_copy(src, dst, lsem.at[i])

    def columns(half, zz):
        return pl.ds(pl.multiple_of(512 * zz + 256 * half, 256), 256)

    loads = [
        load(0, wt, wall.at[z, x]),
        load(1, keys, kv),
        load(2, values, vv),
        load(3, filt, fv),
        load(4, queries, qv),
    ]
    for zz in range(2):
        at = pl.ds(256 * zz, 256)
        loads.append(load(5 + zz, cot.at[:, columns(yl, zz)], cotg.at[0, t, :, at]))
        loads.append(load(7 + zz, cot.at[:, columns(1 - yl, zz)], cots.at[:, at]))
    for one in loads:
        one.start()

    barrier = pltpu.get_barrier_semaphore()

    def greet(i, carry):
        pl.semaphore_signal(barrier, inc=1, device_id={"seq": lax.rem(s + i, NS)}, device_id_type=MESH)
        return carry

    lax.fori_loop(1, NS, greet, 0)
    for i in range(1, 4):
        pl.semaphore_signal(barrier, inc=1, device_id={"tp": lax.rem(t + i, 4)}, device_id_type=MESH)
    pl.semaphore_signal(barrier, inc=1, device_id={"seq": beside, "tp": far}, device_id_type=MESH)

    def rows_out(val, dst, at, c):
        moved = val.T.astype(BF).reshape(8, OWN, TOK)
        if at is None:
            dst[pl.ds(8 * c, 8)] = moved
        else:
            dst[pl.ds(8 * c, 8), at] = moved

    def lanes(c):
        return pl.ds(pl.multiple_of(c * 128, 128), 128)

    def loop(n, body):
        def step(i, carry):
            body(i)
            return carry

        lax.fori_loop(0, n, step, 0)

    loads[1].wait()
    loads[2].wait()

    def mix(c):
        at = lanes(c)
        rows_out(kv[:, at].astype(F32) * vv[:, at].astype(F32), xs, None, c)

    loop(8, mix)
    for i in (0, 5, 6, 7, 8):
        loads[i].wait()

    pl.semaphore_wait(barrier, NS - 1 + 3 + 1)

    def remote(src, dst, ss, rs, **to):
        return pltpu.make_async_remote_copy(
            src_ref=src, dst_ref=dst, send_sem=ss, recv_sem=rs, device_id=to, device_id_type=MESH
        )

    def send_all(i, src, dst):
        def one(k, carry):
            d = lax.rem(s + k, NS)
            remote(src.at[d], dst.at[s], a2s.at[i], a2r.at[i], seq=d).start()
            return carry

        pltpu.make_async_copy(src.at[s], dst.at[s], a2l.at[i]).start()
        lax.fori_loop(1, NS, one, 0)

    def wait_all(i, src, dst):
        remote(src.at[pl.ds(0, NS - 1)], dst.at[pl.ds(0, NS - 1)], a2s.at[i], a2r.at[i], seq=s).wait_recv()
        pltpu.make_async_copy(src.at[s], dst.at[s], a2l.at[i]).wait()

    def zdev(k):
        return lax.rem(z + k + NZ, NZ)

    def zcopy(k, way):
        src = wall.at[zdev(-k * way), x]
        if k == 3:
            src = wall.at[zdev(-k * way), x, pl.ds(0 if way > 0 else FEAT // 2, FEAT // 2)]
        i = 0 if way > 0 else 1
        return remote(src, src, zs.at[i, k], zr.at[i, k], seq=zdev(way) * NR + r)

    def zwait(k):
        for i, way in ((0, 1), (1, -1)):
            src = wall.at[zdev(-(k + 1) * way), x]
            if k == 3:
                src = wall.at[zdev(-(k + 1) * way), x, pl.ds(0 if way > 0 else FEAT // 2, FEAT // 2)]
            remote(src, src, zs.at[i, k], zr.at[i, k], seq=zdev(way) * NR + r).wait_recv()

    def zstart(k):
        zcopy(k, 1).start()
        zcopy(k, -1).start()

    batches = ((0,), (-1, 1), (-2, 2), (-3, 3), (4,))

    def xdev(k):
        return lax.rem(x + k + NX, NX)

    def xcopy(off, way, back=False):
        i, j = off + 3, 0 if way > 0 else 1
        ref = wall.at[zdev(off), xdev(-way if back else 0)]
        return remote(ref, ref, ws.at[i, j], wr.at[i, j], seq=z * NR + yl * NX + xdev(way))

    def xfwd(off, way, back=False):
        i, j = off + 3, 0 if way > 0 else 1
        half = pl.ds(0 if way > 0 else FEAT // 2, FEAT // 2)
        ref = wall.at[zdev(off), xdev(-2 * way if back else -way), half]
        return remote(ref, ref, wfs.at[i, j], wfr.at[i, j], seq=z * NR + yl * NX + xdev(way))

    def xstart(k):
        for off in batches[k]:
            xcopy(off, 1).start()
            xcopy(off, -1).start()

    def xpass(k):
        for off in batches[k]:
            for way in (1, -1):
                xcopy(off, way, True).wait_recv()
                xfwd(off, way).start()

    def xwait(k):
        for off in batches[k]:
            for way in (1, -1):
                xfwd(off, way, True).wait_recv()

    def forward(src, dst):
        def widen(m):
            wide = src[pl.ds(8 * m, 8)].reshape(128, TOK).astype(F32)
            for lane in range(2):
                s32[lane, pl.ds(128 * m, 128)] = wide[:, 128 * lane : 128 * lane + 128]

        loop(8, widen)
        for c in range(OWN):
            at = pl.ds(c, NS, stride=OWN)
            taken = jnp.concatenate([s32[lane, at, :] for lane in range(2)], 1).astype(BF)
            y = jnp.dot(wb[...], taken, preferred_element_type=F32)
            re, im = y[:NS], y[NS:]
            tre = re * cosr[...] + im * sinr[...]
            tim = im * cosr[...] - re * sinr[...]
            for lane in range(2):
                t32[lane, at, :] = tre[:, 128 * lane : 128 * lane + 128]
                t32[2 + lane, at, :] = tim[:, 128 * lane : 128 * lane + 128]

        def second(m):
            at = pl.ds(128 * m, 128)
            left = jnp.concatenate([t32[lane, at] for lane in range(4)], 1).astype(BF)
            dst[at] = jnp.dot(left, dfa[...], preferred_element_type=F32).astype(BF)

        loop(8, second)

    def filter_at(m):
        at = pl.ds(8 * m, 8)
        return fr[at, 0].reshape(128, TOK).astype(F32), fr[at, 1].reshape(128, TOK).astype(F32)

    def inverse(src, conj, dst):
        def first(m):
            at = pl.ds(128 * m, 128)
            sre, sim = src[at, 0:TOK].astype(F32), src[at, TOK:].astype(F32)
            fre, fim = filter_at(m)
            if conj:
                fim = -fim
            y = jnp.concatenate([sre * fre - sim * fim, sre * fim + sim * fre], 1).astype(BF)
            o = jnp.dot(y, dia[...], preferred_element_type=F32)
            for lane in range(4):
                t32[lane, at] = o[:, 128 * lane : 128 * lane + 128]

        loop(8, first)
        for c in range(OWN):
            at = pl.ds(c, NS, stride=OWN)
            re = jnp.concatenate([t32[lane, at, :] for lane in range(2)], 1)
            im = jnp.concatenate([t32[2 + lane, at, :] for lane in range(2)], 1)
            tre = re * cosr[...] - im * sinr[...]
            tim = im * cosr[...] + re * sinr[...]
            both = jnp.concatenate([tre, tim], 0).astype(BF)
            o = jnp.dot(wbi[...], both, preferred_element_type=F32) * (1.0 / LENGTH)
            for lane in range(2):
                s32[lane, at, :] = o[:, 128 * lane : 128 * lane + 128]

        def narrow(m):
            wide = jnp.concatenate([s32[lane, pl.ds(128 * m, 128)] for lane in range(2)], 1)
            dst[pl.ds(8 * m, 8)] = wide.astype(BF).reshape(8, OWN, TOK)

        loop(8, narrow)

    def back_at(src, c):
        return src[pl.ds(8 * c, 8)].reshape(128, TOK).astype(F32).T

    zstart(0)
    xstart(0)
    half_sib = remote(cotg.at[0, t], cotg.at[0, t], ts.at[0], tr.at[0], tp=sib)
    half_far = remote(cotg.at[0, t], cotg.at[0, t], ts.at[1], tr.at[1], tp=far)
    half_beside = remote(cots, cotg.at[1, t], ts.at[2], tr.at[2], seq=beside)
    half_across = remote(cots, cotg.at[1, t], ts.at[3], tr.at[3], seq=beside, tp=far)
    send_all(0, xs, xr)
    for copy in (half_sib, half_far, half_beside, half_across):
        copy.start()
    zwait(0)
    zstart(1)
    xstart(1)
    loads[3].wait()

    def turn_filter(c):
        at = lanes(c)
        for p in range(2):
            rows_out(fv[p, :, at], fs, p, c)

    loop(4, turn_filter)
    zwait(1)
    zstart(2)
    xstart(2)
    xpass(0)
    loop(4, lambda c: turn_filter(c + 4))
    zwait(2)
    zstart(3)
    xstart(3)
    xpass(1)
    zwait(3)
    xstart(4)
    send_all(1, fs, fr)
    xpass(2)
    arrived = []
    for i, (tok, blk) in enumerate(((0, far), (1, t), (1, far))):
        ref = cotg.at[tok, blk]
        remote(ref, ref, ts.at[1 + i], tr.at[1 + i], tp=sib).wait_recv()
        on = remote(ref, ref, ts.at[4 + i], tr.at[4 + i], tp=sib)
        on.start()
        arrived.append(on)
    xpass(3)

    wait_all(0, xs, xr)
    forward(xr, spec)
    xpass(4)
    for i, (tok, blk) in ((0, (0, sib)), (4, (0, fars)), (5, (1, sib)), (6, (1, fars))):
        ref = cotg.at[tok, blk]
        remote(ref, ref, ts.at[i], tr.at[i], tp=sib).wait_recv()
    wait_all(1, fs, fr)
    inverse(spec, False, cs)
    send_all(2, cs, cr)
    for k in range(5):
        xwait(k)

    def quarter(n):
        return pl.ds(256 * n, 256)

    def grad_half(tok, n):
        total = None
        for blk in range(4):
            right = wall[2 * blk : 2 * blk + 2, :, :, quarter(n)].reshape(512, 256)
            y = jnp.dot(cotg[tok, blk], right, preferred_element_type=F32)
            total = y if total is None else total + y
        return total

    def grad_copy(n):
        return remote(gsend.at[:, quarter(n)], grecv.at[:, quarter(n)], gs.at[n], gr.at[n], seq=beside)

    for n in range(4):
        gsend[:, quarter(n)] = grad_half(1, n).astype(BF)
        grad_copy(n).start()
    for n in range(4):
        gg[:, quarter(n)] = grad_half(0, n)
    loads[4].wait()

    def turn_grad(c):
        at = lanes(c)
        y = gg[:, at] + grecv[:, at].astype(F32)
        gg[:, at] = y
        rows_out(y * qv[:, at].astype(F32), gcs, None, c)

    for n in range(4):
        grad_copy(n).wait_recv()
        turn_grad(2 * n)
        turn_grad(2 * n + 1)
    send_all(3, gcs, gcr)

    wait_all(2, cs, cr)

    def gate(c):
        at = lanes(c)
        y = back_at(cr, c).astype(BF)
        yf = y.astype(F32)
        stage[0, :, at] = (gg[:, at] * yf).astype(BF)
        gat[0, :, at] = (qv[:, at].astype(F32) * yf).astype(BF)

    loop(8, gate)
    gat_copy = remote(gat.at[0], gat.at[1], ts.at[7], tr.at[7], seq=beside)
    gat_copy.start()
    gq_out = pltpu.make_async_copy(stage.at[0], gq, osem.at[0])
    gq_out.start()

    def out_blocks(tok):
        def one(blk):
            for zz in range(2):
                right = wall[2 * blk + zz].reshape(256, CH)
                part[tok, blk, :, pl.ds(256 * zz, 256)] = lax.dot_general(
                    gat[tok], right, (((1,), (1,)), ((), ())), preferred_element_type=F32
                ).astype(BF)

        loop(4, one)

    out_blocks(0)

    wait_all(3, gcs, gcr)
    forward(gcr, gspec)

    def grad_filter(m):
        at = pl.ds(128 * m, 128)
        xre, xim = spec[at, 0:TOK].astype(F32), spec[at, TOK:].astype(F32)
        gre, gim = gspec[at, 0:TOK].astype(F32), gspec[at, TOK:].astype(F32)
        scale = 1.0 / LENGTH
        gfs[pl.ds(8 * m, 8), 0] = ((xre * gre + xim * gim) * scale).astype(BF).reshape(8, OWN, TOK)
        gfs[pl.ds(8 * m, 8), 1] = ((xre * gim - xim * gre) * scale).astype(BF).reshape(8, OWN, TOK)

    loop(8, grad_filter)
    send_all(4, gfs, gfr)
    inverse(gspec, True, gms)
    send_all(5, gms, gmr)

    gat_copy.wait_recv()
    out_blocks(1)

    def core_copy(tok, hh):
        i = 2 * tok + hh
        return remote(part.at[tok, hh * 2 + (1 - core)], prec.at[tok, hh], ps.at[i], pr.at[i], tp=sib)

    pairs = ((0, 0), (0, 1), (1, 0), (1, 1))
    for tok, hh in pairs:
        core_copy(tok, hh).start()
    for tok, hh in pairs:
        core_copy(tok, hh).wait_recv()
        ssum[tok, hh] = (part[tok, hh * 2 + core].astype(F32) + prec[tok, hh].astype(F32)).astype(BF)
    sum_far = remote(ssum.at[0, 1 - h], orec.at[0], ts.at[8], tr.at[8], tp=far)
    sum_beside = remote(ssum.at[1, h], orec.at[1], ts.at[9], tr.at[9], seq=beside)
    sum_across = remote(ssum.at[1, 1 - h], orec.at[2], ts.at[10], tr.at[10], seq=beside, tp=far)
    sums = (sum_far, sum_beside, sum_across)
    for copy in sums:
        copy.start()
    for copy in sums:
        copy.wait_recv()
    for zz in range(2):
        at = pl.ds(256 * zz, 256)
        mine = ssum[0, h, :, at].astype(F32) + orec[0, :, at].astype(F32)
        stage[1, :, columns(yl, zz)] = mine.astype(BF)
        other = orec[1, :, at].astype(F32) + orec[2, :, at].astype(F32)
        stage[1, :, columns(1 - yl, zz)] = other.astype(BF)
    out_out = pltpu.make_async_copy(stage.at[1], out, osem.at[1])
    out_out.start()

    wait_all(4, gfs, gfr)
    wait_all(5, gms, gmr)

    for i, src, dst in ((0, xs, xr), (1, fs, fr), (2, cs, cr), (3, gcs, gcr), (4, gfs, gfr), (5, gms, gmr)):
        remote(src.at[pl.ds(0, NS - 1)], dst.at[pl.ds(0, NS - 1)], a2s.at[i], a2r.at[i], seq=s).wait_send()
    for k in range(4):
        zcopy(k, 1).wait_send()
        zcopy(k, -1).wait_send()
    for batch in batches:
        for off in batch:
            for way in (1, -1):
                xcopy(off, way).wait_send()
                xfwd(off, way).wait_send()
    for copy in (half_sib, half_far, half_beside, half_across, *arrived, gat_copy, *sums):
        copy.wait_send()
    for n in range(4):
        grad_copy(n).wait_send()
    for tok, hh in pairs:
        core_copy(tok, hh).wait_send()
    gq_out.wait()
    out_out.wait()


def finish(out_in, gq_in, gfr, gmr, keys, values, out, gq, gk, gv, gf):
    out[...] = out_in[...]
    gq[...] = gq_in[...]
    for p in range(2):
        gf[p] = gfr[:, p].reshape(128, TOK).astype(F32).T
    y = gmr[...].reshape(128, TOK).astype(F32).T
    gk[...] = (y * values[...].astype(F32)).astype(BF)
    gv[...] = (y * keys[...].astype(F32)).astype(BF)


def shards(queries, keys, values, filter_spectrum, weight, cotangent):
    wt = weight.T
    filt = filter_spectrum.reshape(2, TOK, CH)
    anywhere = pl.BlockSpec(memory_space=pl.ANY)
    vmem = pl.BlockSpec(memory_space=pltpu.VMEM)
    flat = jax.ShapeDtypeStruct((TOK, CH), BF)
    blocks = pltpu.VMEM((NS, OWN, TOK), BF)
    pairs = pltpu.VMEM((NS, 2, OWN, TOK), BF)
    whole = pltpu.VMEM((TOK, CH), BF)
    dma = pltpu.SemaphoreType.DMA
    blocks_out = jax.ShapeDtypeStruct((NS, OWN, TOK), BF)
    pairs_out = jax.ShapeDtypeStruct((NS, 2, OWN, TOK), BF)
    out, gq, gfr, gmr = pl.pallas_call(
        kernel,
        out_shape=(flat, flat, pairs_out, blocks_out),
        in_specs=[anywhere] * 6 + [vmem] * 6,
        out_specs=(anywhere,) * 4,
        scratch_shapes=[
            whole, whole, whole,
            pltpu.VMEM((2, 4, TOK, 512), BF),
            pltpu.VMEM((TOK, 512), BF),
            pltpu.VMEM((2, TOK, CH), F32),
            pltpu.VMEM((NZ, NX, FEAT, CH), BF),
            blocks, blocks, pairs, pairs,
            pltpu.VMEM((ROWS, 2 * TOK), BF),
            pltpu.VMEM((ROWS, 2 * TOK), BF),
            pltpu.VMEM((2, ROWS, 128), F32),
            pltpu.VMEM((4, ROWS, 128), F32),
            blocks, blocks, blocks, blocks,
            pairs, blocks,
            pltpu.VMEM((2, TOK, CH), BF),
            pltpu.VMEM((TOK, CH), F32),
            whole, whole,
            pltpu.VMEM((2, 4, TOK, 512), BF),
            pltpu.VMEM((2, 2, TOK, 512), BF),
            pltpu.VMEM((2, 2, TOK, 512), BF),
            pltpu.VMEM((3, TOK, 512), BF),
            pltpu.VMEM((2, TOK, CH), BF),
            dma((9,)), dma((2,)), dma((6,)), dma((6,)), dma((6,)),
            dma((2, 4)), dma((2, 4)), dma((8, 2)), dma((8, 2)), dma((8, 2)), dma((8, 2)),
            dma((11,)), dma((11,)), dma((4,)), dma((4,)), dma((4,)), dma((4,)),
        ],
        compiler_params=pltpu.CompilerParams(
            collective_id=0, has_side_effects=True, vmem_limit_bytes=56 * 1024 * 1024
        ),
    )(keys, values, queries, cotangent, filt, wt, *tables())
    lane = pl.BlockSpec((TOK, 128), lambda c: (0, c))
    out, gq, gk, gv, gf = pl.pallas_call(
        finish,
        grid=(8,),
        out_shape=(flat, flat, flat, flat, jax.ShapeDtypeStruct((2, TOK, CH), F32)),
        in_specs=[
            lane,
            lane,
            pl.BlockSpec((8, 2, OWN, TOK), lambda c: (c, 0, 0, 0)),
            pl.BlockSpec((8, OWN, TOK), lambda c: (c, 0, 0)),
            lane,
            lane,
        ],
        out_specs=(lane, lane, lane, lane, pl.BlockSpec((2, TOK, 128), lambda c: (0, 0, c))),
        compiler_params=pltpu.CompilerParams(vmem_limit_bytes=56 * 1024 * 1024),
    )(out, gq, gfr, gmr, keys, values)
    return out, gq, gk, gv, gf.reshape(2, 1, TOK, CH)


def solution(mesh):
    io = P("seq", "tp")
    spectrum = P(None, "seq", None, "tp")
    return jax.shard_map(
        shards,
        mesh=mesh,
        in_specs=(io, io, io, spectrum, P("tp", "seq"), io),
        out_specs=(io, io, io, io, spectrum),
        check_vma=False,
    )
```

```python
import math

import jax
import jax.numpy as jnp
import numpy as np
from jax import lax
from jax.experimental import pallas as pl
from jax.experimental.pallas import tpu as pltpu
from jax.sharding import PartitionSpec as P

MESH = pl.DeviceIdType.MESH
BF = jnp.bfloat16
F32 = jnp.float32

NZ, NY, NX = 8, 2, 4
NS = NZ * NY * NX
NR = NY * NX
TOK = 256
CH = 1024
OWN = CH // NS
FEAT = 64
LENGTH = TOK * NS
ROWS = NS * OWN


def tables():
    b = np.arange(NS)
    ang = 2.0 * np.pi / NS * (b[:, None] * b[None, :] % NS)
    wb = np.concatenate([np.cos(ang), -np.sin(ang)], 0)
    wbi = np.concatenate([np.cos(ang), -np.sin(ang)], 1)
    a = np.arange(TOK)
    ang = 2.0 * np.pi / TOK * (a[:, None] * a[None, :] % TOK)
    c, s = np.cos(ang), np.sin(ang)
    fwd = np.block([[c, -s], [s, c]])
    inv = np.block([[c, s], [-s, c]])
    ang = 2.0 * np.pi / LENGTH * (b[:, None] * a[None, :] % LENGTH)
    low = [jnp.asarray(t.astype(np.float32)).astype(BF) for t in (wb, wbi, fwd, inv)]
    return (*low, jnp.asarray(np.cos(ang).astype(np.float32)), jnp.asarray(np.sin(ang).astype(np.float32)))


def kernel(
    keys, values, queries, cot, filt, wt, wb_in, wbi_in, dfa_in, dia_in, cos_in, sin_in,
    out, gq, gfr, gmr,
    wb, wbi, dfa, dia, cosr, sinr, kv, vv, qv, cotg, cots, fv, wall, xs, xr, fs, fr, spec, gspec, s32, t32, cs, cr, gcs, gcr, gfs, gms,
    gat, gg, gsend, grecv, part, prec, ssum, orec, stage,
    row_sem, side_sem, lsem, osem, a2s, a2r, a2l, zs, zr, ws, wr, wfs, wfr, ts, tr, gs, gr, ps, pr,
):
    s = lax.axis_index("seq")
    t = lax.axis_index("tp")
    z, r = s // NR, lax.rem(s, NR)
    yl, x = r // NX, lax.rem(r, NX)
    h, core = t // 2, lax.rem(t, 2)
    sib = h * 2 + (1 - core)
    far = (1 - h) * 2 + core
    fars = (1 - h) * 2 + (1 - core)
    beside = z * NR + (1 - yl) * NX + x

    def load(i, src, dst):
        return pltpu.make_async_copy(src, dst, lsem.at[i])

    def columns(half, zz):
        return pl.ds(pl.multiple_of(512 * zz + 256 * half, 256), 256)

    loads = [
        load(0, wt, wall.at[z, x]),
        load(1, keys, kv),
        load(2, values, vv),
        load(3, filt, fv),
        load(4, queries, qv),
    ]
    for zz in range(2):
        at = pl.ds(256 * zz, 256)
        loads.append(load(5 + zz, cot.at[:, columns(yl, zz)], cotg.at[0, t, :, at]))
        loads.append(load(7 + zz, cot.at[:, columns(1 - yl, zz)], cots.at[:, at]))
    tables_in = ((wb_in, wb), (dfa_in, dfa), (cos_in, cosr), (sin_in, sinr), (dia_in, dia), (wbi_in, wbi))
    for i, (src, dst) in enumerate(tables_in):
        loads.append(load(9 + i, src, dst))
    for one in loads:
        one.start()

    barrier = pltpu.get_barrier_semaphore()

    line = [zz_ * NR + r for zz_ in (lax.rem(z + k, NZ) for k in range(1, NZ))]
    row = [z * NR + yl * NX + lax.rem(x + k, NX) for k in range(1, NX)]
    for d in (*line, *row, beside):
        pl.semaphore_signal(barrier, inc=1, device_id={"seq": d}, device_id_type=MESH)
    for i in range(1, 4):
        pl.semaphore_signal(barrier, inc=1, device_id={"tp": lax.rem(t + i, 4)}, device_id_type=MESH)
    pl.semaphore_signal(barrier, inc=1, device_id={"seq": beside, "tp": far}, device_id_type=MESH)

    def rows_out(val, dst, at, c):
        moved = val.T.astype(BF).reshape(8, OWN, TOK)
        if at is None:
            dst[pl.ds(8 * c, 8)] = moved
        else:
            dst[pl.ds(8 * c, 8), at] = moved

    def lanes(c):
        return pl.ds(pl.multiple_of(c * 128, 128), 128)

    def loop(n, body):
        def step(i, carry):
            body(i)
            return carry

        lax.fori_loop(0, n, step, 0)

    def mix(c):
        at = lanes(c)
        rows_out(kv[:, at].astype(F32) * vv[:, at].astype(F32), xs, None, c)

    loads[0].wait()
    for one in loads[5:9]:
        one.wait()

    pl.semaphore_wait(barrier, len(line) + len(row) + 1 + 3 + 1)

    def remote(src, dst, ss, rs, **to):
        return pltpu.make_async_remote_copy(
            src_ref=src, dst_ref=dst, send_sem=ss, recv_sem=rs, device_id=to, device_id_type=MESH
        )

    def owner(block):
        zz = lax.rem(block, 16) // 2
        return zz * NR + lax.rem(block, 2) * NX + lax.rem(block // 16 + zz, NX)

    own = lax.rem(x + NZ - z, NX) * 16 + z * 2 + yl

    def send(i, src, dst, d):
        @pl.when(d != s)
        def _():
            remote(src, dst, a2s.at[i], a2r.at[i], seq=d).start()

        @pl.when(d == s)
        def _():
            pltpu.make_async_copy(src, dst, a2l.at[i]).start()

    def send_owners(i, src, dst, first=0, count=NS):
        def one(k):
            block = first + lax.rem(own + k, count)
            send(i, src.at[block], dst.at[s], owner(block))

        loop(count, one)

    def send_home(i, src, dst, m):
        def one(k):
            d = m * NR + lax.rem(r + k, NR)
            send(i, src.at[d], dst.at[own], d)

        loop(NR, one)

    def ring_z(body):
        loop(NZ, lambda k: body(lax.rem(z + k, NZ)))

    def wait_all(i, src, dst):
        remote(src.at[pl.ds(0, NS - 1)], dst.at[pl.ds(0, NS - 1)], a2s.at[i], a2r.at[i], seq=s).wait_recv()
        pltpu.make_async_copy(src.at[s], dst.at[s], a2l.at[i]).wait()

    def zdev(k):
        return lax.rem(z + k + NZ, NZ)

    def zcopy(k, way):
        src = wall.at[zdev(-k * way), x]
        if k == 3:
            src = wall.at[zdev(-k * way), x, pl.ds(0 if way > 0 else FEAT // 2, FEAT // 2)]
        i = 0 if way > 0 else 1
        return remote(src, src, zs.at[i, k], zr.at[i, k], seq=zdev(way) * NR + r)

    def zwait(k):
        for i, way in ((0, 1), (1, -1)):
            src = wall.at[zdev(-(k + 1) * way), x]
            if k == 3:
                src = wall.at[zdev(-(k + 1) * way), x, pl.ds(0 if way > 0 else FEAT // 2, FEAT // 2)]
            remote(src, src, zs.at[i, k], zr.at[i, k], seq=zdev(way) * NR + r).wait_recv()

    def zstart(k):
        zcopy(k, 1).start()
        zcopy(k, -1).start()

    batches = ((0,), (-1, 1), (-2, 2), (-3, 3), (4,))

    def xdev(k):
        return lax.rem(x + k + NX, NX)

    def xcopy(off, way, back=False):
        i, j = off + 3, 0 if way > 0 else 1
        ref = wall.at[zdev(off), xdev(-way if back else 0)]
        return remote(ref, ref, ws.at[i, j], wr.at[i, j], seq=z * NR + yl * NX + xdev(way))

    def xfwd(off, way, back=False):
        i, j = off + 3, 0 if way > 0 else 1
        half = pl.ds(0 if way > 0 else FEAT // 2, FEAT // 2)
        ref = wall.at[zdev(off), xdev(-2 * way if back else -way), half]
        return remote(ref, ref, wfs.at[i, j], wfr.at[i, j], seq=z * NR + yl * NX + xdev(way))

    def xstart(k):
        for off in batches[k]:
            xcopy(off, 1).start()
            xcopy(off, -1).start()

    def xpass(k):
        for off in batches[k]:
            for way in (1, -1):
                xcopy(off, way, True).wait_recv()
                xfwd(off, way).start()

    def xwait(k):
        for off in batches[k]:
            for way in (1, -1):
                xfwd(off, way, True).wait_recv()

    def forward(src, dst, then=None):
        def widen(m):
            wide = src[pl.ds(8 * m, 8)].reshape(128, TOK).astype(F32)
            for lane in range(2):
                s32[lane, pl.ds(pl.multiple_of(128 * m, 128), 128)] = wide[:, 128 * lane : 128 * lane + 128]

        loop(8, widen)
        for c in range(OWN):
            at = pl.ds(c, NS, stride=OWN)
            taken = jnp.concatenate([s32[lane, at, :] for lane in range(2)], 1).astype(BF)
            y = jnp.dot(wb[...], taken, preferred_element_type=F32)
            re, im = y[:NS], y[NS:]
            tre = re * cosr[...] + im * sinr[...]
            tim = im * cosr[...] - re * sinr[...]
            for lane in range(2):
                t32[lane, at, :] = tre[:, 128 * lane : 128 * lane + 128]
                t32[2 + lane, at, :] = tim[:, 128 * lane : 128 * lane + 128]

        def second(m):
            at = pl.ds(pl.multiple_of(128 * m, 128), 128)
            left = jnp.concatenate([t32[lane, at] for lane in range(4)], 1).astype(BF)
            dst[at] = jnp.dot(left, dfa[...], preferred_element_type=F32).astype(BF)
            if then is not None:
                then(m)

        ring_z(second)

    def filter_at(m):
        at = pl.ds(8 * m, 8)
        return fr[at, 0].reshape(128, TOK).astype(F32), fr[at, 1].reshape(128, TOK).astype(F32)

    def inverse(i, src, conj, dst, there):
        def first(m):
            at = pl.ds(pl.multiple_of(128 * m, 128), 128)
            sre, sim = src[at, 0:TOK].astype(F32), src[at, TOK:].astype(F32)
            fre, fim = filter_at(m)
            if conj:
                fim = -fim
            y = jnp.concatenate([sre * fre - sim * fim, sre * fim + sim * fre], 1).astype(BF)
            o = jnp.dot(y, dia[...], preferred_element_type=F32)
            for lane in range(4):
                t32[lane, at] = o[:, 128 * lane : 128 * lane + 128]

        loop(8, first)
        for c in range(OWN):
            at = pl.ds(c, NS, stride=OWN)
            re = jnp.concatenate([t32[lane, at, :] for lane in range(2)], 1)
            im = jnp.concatenate([t32[2 + lane, at, :] for lane in range(2)], 1)
            tre = re * cosr[...] - im * sinr[...]
            tim = im * cosr[...] + re * sinr[...]
            both = jnp.concatenate([tre, tim], 0).astype(BF)
            o = jnp.dot(wbi[...], both, preferred_element_type=F32) * (1.0 / LENGTH)
            for lane in range(2):
                s32[lane, at, :] = o[:, 128 * lane : 128 * lane + 128]

        def narrow(m):
            wide = jnp.concatenate([s32[lane, pl.ds(pl.multiple_of(128 * m, 128), 128)] for lane in range(2)], 1)
            dst[pl.ds(8 * m, 8)] = wide.astype(BF).reshape(8, OWN, TOK)
            send_home(i, dst, there, m)

        ring_z(narrow)

    def back_at(src, c):
        return src[pl.ds(8 * c, 8)].reshape(128, TOK).astype(F32).T

    zstart(0)
    xstart(0)
    half_sib = remote(cotg.at[0, t], cotg.at[0, t], ts.at[0], tr.at[0], tp=sib)
    half_far = remote(cotg.at[0, t], cotg.at[0, t], ts.at[1], tr.at[1], tp=far)
    half_beside = remote(cots, cotg.at[1, t], ts.at[2], tr.at[2], seq=beside)
    half_across = remote(cots, cotg.at[1, t], ts.at[3], tr.at[3], seq=beside, tp=far)
    for d in row:
        pl.semaphore_signal(row_sem, inc=1, device_id={"seq": d}, device_id_type=MESH)
    for copy in (half_sib, half_far, half_beside, half_across):
        copy.start()
    for one in loads[1:3]:
        one.wait()
    loop(4, mix)
    pl.semaphore_wait(row_sem, len(row))
    pl.semaphore_signal(side_sem, inc=1, device_id={"seq": beside}, device_id_type=MESH)
    loop(4, lambda c: mix(c + 4))
    pl.semaphore_wait(side_sem, 1)
    send_owners(0, xs, xr)
    zwait(0)
    zstart(1)
    xstart(1)
    for one in loads[9:]:
        one.wait()
    loads[3].wait()

    def turn_filter(c):
        at = lanes(c)
        for p in range(2):
            rows_out(fv[p, :, at], fs, p, c)

    loop(4, turn_filter)
    zwait(1)
    zstart(2)
    xstart(2)
    xpass(0)
    loop(4, lambda c: turn_filter(c + 4))
    zwait(2)
    zstart(3)
    xstart(3)
    xpass(1)
    zwait(3)
    xstart(4)
    send_owners(1, fs, fr)
    xpass(2)
    arrived = []
    for i, (tok, blk) in enumerate(((0, far), (1, t), (1, far))):
        ref = cotg.at[tok, blk]
        remote(ref, ref, ts.at[1 + i], tr.at[1 + i], tp=sib).wait_recv()
        on = remote(ref, ref, ts.at[4 + i], tr.at[4 + i], tp=sib)
        on.start()
        arrived.append(on)
    xpass(3)

    wait_all(0, xs, xr)
    forward(xr, spec)
    xpass(4)
    for i, (tok, blk) in ((0, (0, sib)), (4, (0, fars)), (5, (1, sib)), (6, (1, fars))):
        ref = cotg.at[tok, blk]
        remote(ref, ref, ts.at[i], tr.at[i], tp=sib).wait_recv()
    wait_all(1, fs, fr)
    inverse(2, spec, False, cs, cr)
    for k in range(5):
        xwait(k)

    def quarter(n):
        return pl.ds(256 * n, 256)

    def grad_half(tok, n):
        total = None
        for blk in range(4):
            right = wall[2 * blk : 2 * blk + 2, :, :, quarter(n)].reshape(512, 256)
            y = jnp.dot(cotg[tok, blk], right, preferred_element_type=F32)
            total = y if total is None else total + y
        return total

    def grad_copy(n):
        return remote(gsend.at[:, quarter(n)], grecv.at[:, quarter(n)], gs.at[n], gr.at[n], seq=beside)

    for n in range(4):
        gsend[:, quarter(n)] = grad_half(1, n).astype(BF)
        grad_copy(n).start()
    for n in range(4):
        gg[:, quarter(n)] = grad_half(0, n)
    loads[4].wait()

    def turn_grad(c):
        at = lanes(c)
        y = gg[:, at] + grecv[:, at].astype(F32)
        gg[:, at] = y
        rows_out(y * qv[:, at].astype(F32), gcs, None, c)

    for n in range(4):
        grad_copy(n).wait_recv()
        turn_grad(2 * n)
        turn_grad(2 * n + 1)
        send_owners(3, gcs, gcr, 16 * n, 16)

    wait_all(2, cs, cr)

    def gate(c):
        at = lanes(c)
        y = back_at(cr, c).astype(BF)
        yf = y.astype(F32)
        stage[0, :, at] = (gg[:, at] * yf).astype(BF)
        gat[0, :, at] = (qv[:, at].astype(F32) * yf).astype(BF)

    loop(8, gate)
    gat_copy = remote(gat.at[0], gat.at[1], ts.at[7], tr.at[7], seq=beside)
    gat_copy.start()
    gq_out = pltpu.make_async_copy(stage.at[0], gq, osem.at[0])
    gq_out.start()

    def out_blocks(tok):
        def one(blk):
            for zz in range(2):
                right = wall[2 * blk + zz].reshape(256, CH)
                part[tok, blk, :, pl.ds(256 * zz, 256)] = lax.dot_general(
                    gat[tok], right, (((1,), (1,)), ((), ())), preferred_element_type=F32
                ).astype(BF)

        loop(4, one)

    out_blocks(0)

    def grad_filter(m):
        at = pl.ds(pl.multiple_of(128 * m, 128), 128)
        xre, xim = spec[at, 0:TOK].astype(F32), spec[at, TOK:].astype(F32)
        gre, gim = gspec[at, 0:TOK].astype(F32), gspec[at, TOK:].astype(F32)
        scale = 1.0 / LENGTH
        gfs[pl.ds(8 * m, 8), 0] = ((xre * gre + xim * gim) * scale).astype(BF).reshape(8, OWN, TOK)
        gfs[pl.ds(8 * m, 8), 1] = ((xre * gim - xim * gre) * scale).astype(BF).reshape(8, OWN, TOK)
        send_home(4, gfs, gfr, m)

    wait_all(3, gcs, gcr)
    forward(gcr, gspec, grad_filter)
    inverse(5, gspec, True, gms, gmr)

    gat_copy.wait_recv()
    out_blocks(1)

    def core_copy(tok, hh):
        i = 2 * tok + hh
        return remote(part.at[tok, hh * 2 + (1 - core)], prec.at[tok, hh], ps.at[i], pr.at[i], tp=sib)

    pairs = ((0, 0), (0, 1), (1, 0), (1, 1))
    for tok, hh in pairs:
        core_copy(tok, hh).start()
    for tok, hh in pairs:
        core_copy(tok, hh).wait_recv()
        ssum[tok, hh] = (part[tok, hh * 2 + core].astype(F32) + prec[tok, hh].astype(F32)).astype(BF)
    sum_far = remote(ssum.at[0, 1 - h], orec.at[0], ts.at[8], tr.at[8], tp=far)
    sum_beside = remote(ssum.at[1, h], orec.at[1], ts.at[9], tr.at[9], seq=beside)
    sum_across = remote(ssum.at[1, 1 - h], orec.at[2], ts.at[10], tr.at[10], seq=beside, tp=far)
    sums = (sum_far, sum_beside, sum_across)
    for copy in sums:
        copy.start()
    for copy in sums:
        copy.wait_recv()
    for zz in range(2):
        at = pl.ds(256 * zz, 256)
        mine = ssum[0, h, :, at].astype(F32) + orec[0, :, at].astype(F32)
        stage[1, :, columns(yl, zz)] = mine.astype(BF)
        other = orec[1, :, at].astype(F32) + orec[2, :, at].astype(F32)
        stage[1, :, columns(1 - yl, zz)] = other.astype(BF)
    out_out = pltpu.make_async_copy(stage.at[1], out, osem.at[1])
    out_out.start()

    wait_all(4, gfs, gfr)
    wait_all(5, gms, gmr)

    for i, src, dst in ((0, xs, xr), (1, fs, fr), (2, cs, cr), (3, gcs, gcr), (4, gfs, gfr), (5, gms, gmr)):
        remote(src.at[pl.ds(0, NS - 1)], dst.at[pl.ds(0, NS - 1)], a2s.at[i], a2r.at[i], seq=s).wait_send()
    for k in range(4):
        zcopy(k, 1).wait_send()
        zcopy(k, -1).wait_send()
    for batch in batches:
        for off in batch:
            for way in (1, -1):
                xcopy(off, way).wait_send()
                xfwd(off, way).wait_send()
    for copy in (half_sib, half_far, half_beside, half_across, *arrived, gat_copy, *sums):
        copy.wait_send()
    for n in range(4):
        grad_copy(n).wait_send()
    for tok, hh in pairs:
        core_copy(tok, hh).wait_send()
    gq_out.wait()
    out_out.wait()


def finish(out_in, gq_in, gfr, gmr, keys, values, out, gq, gk, gv, gf):
    out[...] = out_in[...]
    gq[...] = gq_in[...]
    for p in range(2):
        gf[p] = gfr[:, p].reshape(-1, TOK).astype(F32).T
    y = gmr[...].reshape(-1, TOK).astype(F32).T
    gk[...] = (y * values[...].astype(F32)).astype(BF)
    gv[...] = (y * keys[...].astype(F32)).astype(BF)


def shards(queries, keys, values, filter_spectrum, weight, cotangent):
    wt = weight.T
    filt = filter_spectrum.reshape(2, TOK, CH)
    anywhere = pl.BlockSpec(memory_space=pl.ANY)
    flat = jax.ShapeDtypeStruct((TOK, CH), BF)
    blocks = pltpu.VMEM((NS, OWN, TOK), BF)
    pairs = pltpu.VMEM((NS, 2, OWN, TOK), BF)
    whole = pltpu.VMEM((TOK, CH), BF)
    dma = pltpu.SemaphoreType.DMA
    blocks_out = jax.ShapeDtypeStruct((NS, OWN, TOK), BF)
    pairs_out = jax.ShapeDtypeStruct((NS, 2, OWN, TOK), BF)
    out, gq, gfr, gmr = pl.pallas_call(
        kernel,
        out_shape=(flat, flat, pairs_out, blocks_out),
        in_specs=[anywhere] * 12,
        out_specs=(anywhere,) * 4,
        scratch_shapes=[
            pltpu.VMEM((2 * NS, NS), BF),
            pltpu.VMEM((NS, 2 * NS), BF),
            pltpu.VMEM((2 * TOK, 2 * TOK), BF),
            pltpu.VMEM((2 * TOK, 2 * TOK), BF),
            pltpu.VMEM((NS, TOK), F32),
            pltpu.VMEM((NS, TOK), F32),
            whole, whole, whole,
            pltpu.VMEM((2, 4, TOK, 512), BF),
            pltpu.VMEM((TOK, 512), BF),
            pltpu.VMEM((2, TOK, CH), F32),
            pltpu.VMEM((NZ, NX, FEAT, CH), BF),
            blocks, blocks, pairs, pairs,
            pltpu.VMEM((ROWS, 2 * TOK), BF),
            pltpu.VMEM((ROWS, 2 * TOK), BF),
            pltpu.VMEM((2, ROWS, 128), F32),
            pltpu.VMEM((4, ROWS, 128), F32),
            blocks, blocks, blocks, blocks,
            pairs, blocks,
            pltpu.VMEM((2, TOK, CH), BF),
            pltpu.VMEM((TOK, CH), F32),
            whole, whole,
            pltpu.VMEM((2, 4, TOK, 512), BF),
            pltpu.VMEM((2, 2, TOK, 512), BF),
            pltpu.VMEM((2, 2, TOK, 512), BF),
            pltpu.VMEM((3, TOK, 512), BF),
            pltpu.VMEM((2, TOK, CH), BF),
            pltpu.SemaphoreType.REGULAR, pltpu.SemaphoreType.REGULAR,
            dma((15,)), dma((2,)), dma((6,)), dma((6,)), dma((6,)),
            dma((2, 4)), dma((2, 4)), dma((8, 2)), dma((8, 2)), dma((8, 2)), dma((8, 2)),
            dma((11,)), dma((11,)), dma((4,)), dma((4,)), dma((4,)), dma((4,)),
        ],
        compiler_params=pltpu.CompilerParams(
            collective_id=0, has_side_effects=True, vmem_limit_bytes=56 * 1024 * 1024
        ),
    )(keys, values, queries, cotangent, filt, wt, *tables())
    lane = pl.BlockSpec((TOK, CH // 2), lambda c: (0, c))
    out, gq, gk, gv, gf = pl.pallas_call(
        finish,
        grid=(2,),
        out_shape=(flat, flat, flat, flat, jax.ShapeDtypeStruct((2, TOK, CH), F32)),
        in_specs=[
            lane,
            lane,
            pl.BlockSpec((NS // 2, 2, OWN, TOK), lambda c: (c, 0, 0, 0)),
            pl.BlockSpec((NS // 2, OWN, TOK), lambda c: (c, 0, 0)),
            lane,
            lane,
        ],
        out_specs=(lane, lane, lane, lane, pl.BlockSpec((2, TOK, CH // 2), lambda c: (0, 0, c))),
        compiler_params=pltpu.CompilerParams(vmem_limit_bytes=56 * 1024 * 1024),
    )(out, gq, gfr, gmr, keys, values)
    return out, gq, gk, gv, gf.reshape(2, 1, TOK, CH)


def solution(mesh):
    io = P("seq", "tp")
    spectrum = P(None, "seq", None, "tp")
    return jax.shard_map(
        shards,
        mesh=mesh,
        in_specs=(io, io, io, spectrum, P("tp", "seq"), io),
        out_specs=(io, io, io, io, spectrum),
        check_vma=False,
    )
```

```python
import math

import jax
import jax.numpy as jnp
import numpy as np
from jax import lax
from jax.experimental import pallas as pl
from jax.experimental.pallas import tpu as pltpu
from jax.sharding import PartitionSpec as P

MESH = pl.DeviceIdType.MESH
BF = jnp.bfloat16
F32 = jnp.float32

NZ, NY, NX = 8, 2, 4
NS = NZ * NY * NX
NR = NY * NX
TOK = 256
CH = 1024
OWN = CH // NS
FEAT = 64
LENGTH = TOK * NS
ROWS = NS * OWN


def tables():
    b = np.arange(NS)
    ang = 2.0 * np.pi / NS * (b[:, None] * b[None, :] % NS)
    wb = np.concatenate([np.cos(ang), -np.sin(ang)], 0)
    wbi = np.concatenate([np.cos(ang), -np.sin(ang)], 1)
    a = np.arange(TOK)
    ang = 2.0 * np.pi / TOK * (a[:, None] * a[None, :] % TOK)
    c, s = np.cos(ang), np.sin(ang)
    fwd = np.block([[c, -s], [s, c]])
    inv = np.block([[c, s], [-s, c]])
    ang = 2.0 * np.pi / LENGTH * (b[:, None] * a[None, :] % LENGTH)
    low = [jnp.asarray(t.astype(np.float32)).astype(BF) for t in (wb, wbi, fwd, inv)]
    return (*low, jnp.asarray(np.cos(ang).astype(np.float32)), jnp.asarray(np.sin(ang).astype(np.float32)))


def kernel(
    keys, values, queries, cot, filt, wt, wb_in, wbi_in, dfa_in, dia_in, cos_in, sin_in,
    out, gq, gfr, gmr,
    wb, wbi, dfa, dia, cosr, sinr, kv, vv, qv, cotg, cots, fv, wall, xs, xr, fs, fr, spec, gspec, s32, t32, cs, cr, gcs, gcr, gfs, gms,
    gat, gg, gsend, grecv, part, prec, ssum, orec, stage,
    row_sem, side_sem, lsem, osem, a2s, a2r, a2l, zs, zr, ws, wr, wfs, wfr, ts, tr, gs, gr, ps, pr,
):
    s = lax.axis_index("seq")
    t = lax.axis_index("tp")
    z, r = s // NR, lax.rem(s, NR)
    yl, x = r // NX, lax.rem(r, NX)
    h, core = t // 2, lax.rem(t, 2)
    sib = h * 2 + (1 - core)
    far = (1 - h) * 2 + core
    fars = (1 - h) * 2 + (1 - core)
    beside = z * NR + (1 - yl) * NX + x

    def load(i, src, dst):
        return pltpu.make_async_copy(src, dst, lsem.at[i])

    def columns(half, zz):
        return pl.ds(pl.multiple_of(512 * zz + 256 * half, 256), 256)

    loads = [
        load(0, wt, wall.at[z, x]),
        load(1, keys, kv),
        load(2, values, vv),
        load(3, filt, fv),
        load(4, queries, qv),
    ]
    for zz in range(2):
        at = pl.ds(256 * zz, 256)
        loads.append(load(5 + zz, cot.at[:, columns(yl, zz)], cotg.at[0, t, :, at]))
        loads.append(load(7 + zz, cot.at[:, columns(1 - yl, zz)], cots.at[:, at]))
    tables_in = ((wb_in, wb), (dfa_in, dfa), (cos_in, cosr), (sin_in, sinr), (dia_in, dia), (wbi_in, wbi))
    for i, (src, dst) in enumerate(tables_in):
        loads.append(load(9 + i, src, dst))
    for one in loads:
        one.start()

    barrier = pltpu.get_barrier_semaphore()

    line = [zz_ * NR + r for zz_ in (lax.rem(z + k, NZ) for k in range(1, NZ))]
    row = [z * NR + yl * NX + lax.rem(x + k, NX) for k in range(1, NX)]
    for d in (*line, *row, beside):
        pl.semaphore_signal(barrier, inc=1, device_id={"seq": d}, device_id_type=MESH)
    for i in range(1, 4):
        pl.semaphore_signal(barrier, inc=1, device_id={"tp": lax.rem(t + i, 4)}, device_id_type=MESH)
    pl.semaphore_signal(barrier, inc=1, device_id={"seq": beside, "tp": far}, device_id_type=MESH)

    def rows_out(val, dst, at, c):
        moved = val.T.astype(BF).reshape(8, OWN, TOK)
        if at is None:
            dst[pl.ds(8 * c, 8)] = moved
        else:
            dst[pl.ds(8 * c, 8), at] = moved

    def lanes(c):
        return pl.ds(pl.multiple_of(c * 128, 128), 128)

    def loop(n, body):
        def step(i, carry):
            body(i)
            return carry

        lax.fori_loop(0, n, step, 0, unroll=4)

    def mix(c):
        at = lanes(c)
        rows_out(kv[:, at].astype(F32) * vv[:, at].astype(F32), xs, None, c)

    loads[0].wait()
    for one in loads[5:9]:
        one.wait()

    pl.semaphore_wait(barrier, len(line) + len(row) + 1 + 3 + 1)

    def remote(src, dst, ss, rs, **to):
        return pltpu.make_async_remote_copy(
            src_ref=src, dst_ref=dst, send_sem=ss, recv_sem=rs, device_id=to, device_id_type=MESH
        )

    def owner(block):
        zz = lax.rem(block, 16) // 2
        return zz * NR + lax.rem(block, 2) * NX + lax.rem(block // 16 + zz, NX)

    own = lax.rem(x + NZ - z, NX) * 16 + z * 2 + yl

    def send(i, src, dst, d):
        @pl.when(d != s)
        def _():
            remote(src, dst, a2s.at[i], a2r.at[i], seq=d).start()

        @pl.when(d == s)
        def _():
            pltpu.make_async_copy(src, dst, a2l.at[i]).start()

    def send_owners(i, src, dst, first=0, count=NS):
        def one(k):
            block = first + lax.rem(own + k, count)
            send(i, src.at[block], dst.at[s], owner(block))

        loop(count, one)

    def send_home(i, src, dst, m):
        def one(k):
            d = m * NR + lax.rem(r + k, NR)
            send(i, src.at[d], dst.at[own], d)

        loop(NR, one)

    def ring_z(body):
        for k in (0, 4, 1, 7, 2, 6, 3, 5):
            body(lax.rem(z + k, NZ))

    def wait_all(i, src, dst):
        remote(src.at[pl.ds(0, NS - 1)], dst.at[pl.ds(0, NS - 1)], a2s.at[i], a2r.at[i], seq=s).wait_recv()
        pltpu.make_async_copy(src.at[s], dst.at[s], a2l.at[i]).wait()

    def zdev(k):
        return lax.rem(z + k + NZ, NZ)

    def zcopy(k, way):
        src = wall.at[zdev(-k * way), x]
        if k == 3:
            src = wall.at[zdev(-k * way), x, pl.ds(0 if way > 0 else FEAT // 2, FEAT // 2)]
        i = 0 if way > 0 else 1
        return remote(src, src, zs.at[i, k], zr.at[i, k], seq=zdev(way) * NR + r)

    def zwait(k):
        for i, way in ((0, 1), (1, -1)):
            src = wall.at[zdev(-(k + 1) * way), x]
            if k == 3:
                src = wall.at[zdev(-(k + 1) * way), x, pl.ds(0 if way > 0 else FEAT // 2, FEAT // 2)]
            remote(src, src, zs.at[i, k], zr.at[i, k], seq=zdev(way) * NR + r).wait_recv()

    def zstart(k):
        zcopy(k, 1).start()
        zcopy(k, -1).start()

    batches = ((0,), (-1, 1), (-2, 2), (-3, 3), (4,))

    def xdev(k):
        return lax.rem(x + k + NX, NX)

    def xcopy(off, way, back=False):
        i, j = off + 3, 0 if way > 0 else 1
        ref = wall.at[zdev(off), xdev(-way if back else 0)]
        return remote(ref, ref, ws.at[i, j], wr.at[i, j], seq=z * NR + yl * NX + xdev(way))

    def xfwd(off, way, back=False):
        i, j = off + 3, 0 if way > 0 else 1
        half = pl.ds(0 if way > 0 else FEAT // 2, FEAT // 2)
        ref = wall.at[zdev(off), xdev(-2 * way if back else -way), half]
        return remote(ref, ref, wfs.at[i, j], wfr.at[i, j], seq=z * NR + yl * NX + xdev(way))

    def xstart(k):
        for off in batches[k]:
            xcopy(off, 1).start()
            xcopy(off, -1).start()

    def xpass(k):
        for off in batches[k]:
            for way in (1, -1):
                xcopy(off, way, True).wait_recv()
                xfwd(off, way).start()

    def xwait(k):
        for off in batches[k]:
            for way in (1, -1):
                xfwd(off, way, True).wait_recv()

    def forward(src, dst, then=None):
        def widen(m):
            wide = src[pl.ds(8 * m, 8)].reshape(128, TOK).astype(F32)
            for lane in range(2):
                s32[lane, pl.ds(pl.multiple_of(128 * m, 128), 128)] = wide[:, 128 * lane : 128 * lane + 128]

        loop(8, widen)
        for c in range(OWN):
            at = pl.ds(c, NS, stride=OWN)
            taken = jnp.concatenate([s32[lane, at, :] for lane in range(2)], 1).astype(BF)
            y = jnp.dot(wb[...], taken, preferred_element_type=F32)
            re, im = y[:NS], y[NS:]
            tre = re * cosr[...] + im * sinr[...]
            tim = im * cosr[...] - re * sinr[...]
            for lane in range(2):
                t32[lane, at, :] = tre[:, 128 * lane : 128 * lane + 128]
                t32[2 + lane, at, :] = tim[:, 128 * lane : 128 * lane + 128]

        def second(m):
            at = pl.ds(pl.multiple_of(128 * m, 128), 128)
            left = jnp.concatenate([t32[lane, at] for lane in range(4)], 1).astype(BF)
            dst[at] = jnp.dot(left, dfa[...], preferred_element_type=F32).astype(BF)
            if then is not None:
                then(m)

        ring_z(second)

    def filter_at(m):
        at = pl.ds(8 * m, 8)
        return fr[at, 0].reshape(128, TOK).astype(F32), fr[at, 1].reshape(128, TOK).astype(F32)

    def inverse(i, src, conj, dst, there):
        def first(m):
            at = pl.ds(pl.multiple_of(128 * m, 128), 128)
            sre, sim = src[at, 0:TOK].astype(F32), src[at, TOK:].astype(F32)
            fre, fim = filter_at(m)
            if conj:
                fim = -fim
            y = jnp.concatenate([sre * fre - sim * fim, sre * fim + sim * fre], 1).astype(BF)
            o = jnp.dot(y, dia[...], preferred_element_type=F32)
            for lane in range(4):
                t32[lane, at] = o[:, 128 * lane : 128 * lane + 128]

        loop(8, first)
        for c in range(OWN):
            at = pl.ds(c, NS, stride=OWN)
            re = jnp.concatenate([t32[lane, at, :] for lane in range(2)], 1)
            im = jnp.concatenate([t32[2 + lane, at, :] for lane in range(2)], 1)
            tre = re * cosr[...] - im * sinr[...]
            tim = im * cosr[...] + re * sinr[...]
            both = jnp.concatenate([tre, tim], 0).astype(BF)
            o = jnp.dot(wbi[...], both, preferred_element_type=F32) * (1.0 / LENGTH)
            for lane in range(2):
                s32[lane, at, :] = o[:, 128 * lane : 128 * lane + 128]

        def narrow(m):
            wide = jnp.concatenate([s32[lane, pl.ds(pl.multiple_of(128 * m, 128), 128)] for lane in range(2)], 1)
            dst[pl.ds(8 * m, 8)] = wide.astype(BF).reshape(8, OWN, TOK)
            send_home(i, dst, there, m)

        ring_z(narrow)

    def back_at(src, c):
        return src[pl.ds(8 * c, 8)].reshape(128, TOK).astype(F32).T

    zstart(0)
    xstart(0)
    half_sib = remote(cotg.at[0, t], cotg.at[0, t], ts.at[0], tr.at[0], tp=sib)
    half_far = remote(cotg.at[0, t], cotg.at[0, t], ts.at[1], tr.at[1], tp=far)
    half_beside = remote(cots, cotg.at[1, t], ts.at[2], tr.at[2], seq=beside)
    half_across = remote(cots, cotg.at[1, t], ts.at[3], tr.at[3], seq=beside, tp=far)
    for d in row:
        pl.semaphore_signal(row_sem, inc=1, device_id={"seq": d}, device_id_type=MESH)
    for copy in (half_sib, half_far, half_beside, half_across):
        copy.start()
    for one in loads[1:3]:
        one.wait()
    loop(4, mix)
    pl.semaphore_wait(row_sem, len(row))
    pl.semaphore_signal(side_sem, inc=1, device_id={"seq": beside}, device_id_type=MESH)
    loop(4, lambda c: mix(c + 4))
    pl.semaphore_wait(side_sem, 1)
    send_owners(0, xs, xr)
    zwait(0)
    zstart(1)
    xstart(1)
    for one in loads[9:]:
        one.wait()
    loads[3].wait()

    def turn_filter(c):
        at = lanes(c)
        for p in range(2):
            rows_out(fv[p, :, at], fs, p, c)

    loop(4, turn_filter)
    zwait(1)
    zstart(2)
    xstart(2)
    xpass(0)
    loop(4, lambda c: turn_filter(c + 4))
    send_owners(1, fs, fr)
    zwait(2)
    zstart(3)
    xstart(3)
    xpass(1)
    zwait(3)
    xstart(4)
    xpass(2)
    arrived = []
    for i, (tok, blk) in enumerate(((0, far), (1, t), (1, far))):
        ref = cotg.at[tok, blk]
        remote(ref, ref, ts.at[1 + i], tr.at[1 + i], tp=sib).wait_recv()
        on = remote(ref, ref, ts.at[4 + i], tr.at[4 + i], tp=sib)
        on.start()
        arrived.append(on)
    xpass(3)

    wait_all(0, xs, xr)
    forward(xr, spec)
    xpass(4)
    for i, (tok, blk) in ((0, (0, sib)), (4, (0, fars)), (5, (1, sib)), (6, (1, fars))):
        ref = cotg.at[tok, blk]
        remote(ref, ref, ts.at[i], tr.at[i], tp=sib).wait_recv()
    wait_all(1, fs, fr)
    inverse(2, spec, False, cs, cr)
    for k in range(5):
        xwait(k)

    def quarter(n):
        return pl.ds(256 * n, 256)

    def grad_half(tok, n):
        total = None
        for blk in range(4):
            right = wall[2 * blk : 2 * blk + 2, :, :, quarter(n)].reshape(512, 256)
            y = jnp.dot(cotg[tok, blk], right, preferred_element_type=F32)
            total = y if total is None else total + y
        return total

    def grad_copy(n):
        return remote(gsend.at[:, quarter(n)], grecv.at[:, quarter(n)], gs.at[n], gr.at[n], seq=beside)

    for n in range(4):
        gsend[:, quarter(n)] = grad_half(1, n).astype(BF)
        grad_copy(n).start()
    for n in range(4):
        gg[:, quarter(n)] = grad_half(0, n)
    loads[4].wait()

    def turn_grad(c):
        at = lanes(c)
        y = gg[:, at] + grecv[:, at].astype(F32)
        gg[:, at] = y
        rows_out(y * qv[:, at].astype(F32), gcs, None, c)

    for n in range(4):
        grad_copy(n).wait_recv()
        turn_grad(2 * n)
        turn_grad(2 * n + 1)
        send_owners(3, gcs, gcr, 16 * n, 16)

    wait_all(2, cs, cr)

    def gate(c):
        at = lanes(c)
        y = back_at(cr, c).astype(BF)
        yf = y.astype(F32)
        stage[0, :, at] = (gg[:, at] * yf).astype(BF)
        gat[0, :, at] = (qv[:, at].astype(F32) * yf).astype(BF)

    loop(8, gate)
    gat_copy = remote(gat.at[0], gat.at[1], ts.at[7], tr.at[7], seq=beside)
    gat_copy.start()
    gq_out = pltpu.make_async_copy(stage.at[0], gq, osem.at[0])
    gq_out.start()

    def out_blocks(tok):
        def one(blk):
            for zz in range(2):
                right = wall[2 * blk + zz].reshape(256, CH)
                part[tok, blk, :, pl.ds(256 * zz, 256)] = lax.dot_general(
                    gat[tok], right, (((1,), (1,)), ((), ())), preferred_element_type=F32
                ).astype(BF)

        loop(4, one)

    out_blocks(0)

    def grad_filter(m):
        at = pl.ds(pl.multiple_of(128 * m, 128), 128)
        xre, xim = spec[at, 0:TOK].astype(F32), spec[at, TOK:].astype(F32)
        gre, gim = gspec[at, 0:TOK].astype(F32), gspec[at, TOK:].astype(F32)
        scale = 1.0 / LENGTH
        gfs[pl.ds(8 * m, 8), 0] = ((xre * gre + xim * gim) * scale).astype(BF).reshape(8, OWN, TOK)
        gfs[pl.ds(8 * m, 8), 1] = ((xre * gim - xim * gre) * scale).astype(BF).reshape(8, OWN, TOK)
        send_home(4, gfs, gfr, m)

    wait_all(3, gcs, gcr)
    forward(gcr, gspec, grad_filter)
    inverse(5, gspec, True, gms, gmr)

    gat_copy.wait_recv()
    out_blocks(1)

    def core_copy(tok, hh):
        i = 2 * tok + hh
        return remote(part.at[tok, hh * 2 + (1 - core)], prec.at[tok, hh], ps.at[i], pr.at[i], tp=sib)

    pairs = ((0, 0), (0, 1), (1, 0), (1, 1))
    for tok, hh in pairs:
        core_copy(tok, hh).start()
    for tok, hh in pairs:
        core_copy(tok, hh).wait_recv()
        ssum[tok, hh] = (part[tok, hh * 2 + core].astype(F32) + prec[tok, hh].astype(F32)).astype(BF)
    sum_far = remote(ssum.at[0, 1 - h], orec.at[0], ts.at[8], tr.at[8], tp=far)
    sum_beside = remote(ssum.at[1, h], orec.at[1], ts.at[9], tr.at[9], seq=beside)
    sum_across = remote(ssum.at[1, 1 - h], orec.at[2], ts.at[10], tr.at[10], seq=beside, tp=far)
    sums = (sum_far, sum_beside, sum_across)
    for copy in sums:
        copy.start()
    for copy in sums:
        copy.wait_recv()
    for zz in range(2):
        at = pl.ds(256 * zz, 256)
        mine = ssum[0, h, :, at].astype(F32) + orec[0, :, at].astype(F32)
        stage[1, :, columns(yl, zz)] = mine.astype(BF)
        other = orec[1, :, at].astype(F32) + orec[2, :, at].astype(F32)
        stage[1, :, columns(1 - yl, zz)] = other.astype(BF)
    out_out = pltpu.make_async_copy(stage.at[1], out, osem.at[1])
    out_out.start()

    wait_all(4, gfs, gfr)
    wait_all(5, gms, gmr)

    for i, src, dst in ((0, xs, xr), (1, fs, fr), (2, cs, cr), (3, gcs, gcr), (4, gfs, gfr), (5, gms, gmr)):
        remote(src.at[pl.ds(0, NS - 1)], dst.at[pl.ds(0, NS - 1)], a2s.at[i], a2r.at[i], seq=s).wait_send()
    for k in range(4):
        zcopy(k, 1).wait_send()
        zcopy(k, -1).wait_send()
    for batch in batches:
        for off in batch:
            for way in (1, -1):
                xcopy(off, way).wait_send()
                xfwd(off, way).wait_send()
    for copy in (half_sib, half_far, half_beside, half_across, *arrived, gat_copy, *sums):
        copy.wait_send()
    for n in range(4):
        grad_copy(n).wait_send()
    for tok, hh in pairs:
        core_copy(tok, hh).wait_send()
    gq_out.wait()
    out_out.wait()


def finish(out_in, gq_in, gfr, gmr, keys, values, out, gq, gk, gv, gf):
    out[...] = out_in[...]
    gq[...] = gq_in[...]
    for p in range(2):
        gf[p] = gfr[:, p].reshape(-1, TOK).astype(F32).T
    y = gmr[...].reshape(-1, TOK).astype(F32).T
    gk[...] = (y * values[...].astype(F32)).astype(BF)
    gv[...] = (y * keys[...].astype(F32)).astype(BF)


def shards(queries, keys, values, filter_spectrum, weight, cotangent):
    wt = weight.T
    filt = filter_spectrum.reshape(2, TOK, CH)
    anywhere = pl.BlockSpec(memory_space=pl.ANY)
    flat = jax.ShapeDtypeStruct((TOK, CH), BF)
    blocks = pltpu.VMEM((NS, OWN, TOK), BF)
    pairs = pltpu.VMEM((NS, 2, OWN, TOK), BF)
    whole = pltpu.VMEM((TOK, CH), BF)
    dma = pltpu.SemaphoreType.DMA
    blocks_out = jax.ShapeDtypeStruct((NS, OWN, TOK), BF)
    pairs_out = jax.ShapeDtypeStruct((NS, 2, OWN, TOK), BF)
    out, gq, gfr, gmr = pl.pallas_call(
        kernel,
        out_shape=(flat, flat, pairs_out, blocks_out),
        in_specs=[anywhere] * 12,
        out_specs=(anywhere,) * 4,
        scratch_shapes=[
            pltpu.VMEM((2 * NS, NS), BF),
            pltpu.VMEM((NS, 2 * NS), BF),
            pltpu.VMEM((2 * TOK, 2 * TOK), BF),
            pltpu.VMEM((2 * TOK, 2 * TOK), BF),
            pltpu.VMEM((NS, TOK), F32),
            pltpu.VMEM((NS, TOK), F32),
            whole, whole, whole,
            pltpu.VMEM((2, 4, TOK, 512), BF),
            pltpu.VMEM((TOK, 512), BF),
            pltpu.VMEM((2, TOK, CH), F32),
            pltpu.VMEM((NZ, NX, FEAT, CH), BF),
            blocks, blocks, pairs, pairs,
            pltpu.VMEM((ROWS, 2 * TOK), BF),
            pltpu.VMEM((ROWS, 2 * TOK), BF),
            pltpu.VMEM((2, ROWS, 128), F32),
            pltpu.VMEM((4, ROWS, 128), F32),
            blocks, blocks, blocks, blocks,
            pairs, blocks,
            pltpu.VMEM((2, TOK, CH), BF),
            pltpu.VMEM((TOK, CH), F32),
            whole, whole,
            pltpu.VMEM((2, 4, TOK, 512), BF),
            pltpu.VMEM((2, 2, TOK, 512), BF),
            pltpu.VMEM((2, 2, TOK, 512), BF),
            pltpu.VMEM((3, TOK, 512), BF),
            pltpu.VMEM((2, TOK, CH), BF),
            pltpu.SemaphoreType.REGULAR, pltpu.SemaphoreType.REGULAR,
            dma((15,)), dma((2,)), dma((6,)), dma((6,)), dma((6,)),
            dma((2, 4)), dma((2, 4)), dma((8, 2)), dma((8, 2)), dma((8, 2)), dma((8, 2)),
            dma((11,)), dma((11,)), dma((4,)), dma((4,)), dma((4,)), dma((4,)),
        ],
        compiler_params=pltpu.CompilerParams(
            collective_id=0, has_side_effects=True, vmem_limit_bytes=56 * 1024 * 1024
        ),
    )(keys, values, queries, cotangent, filt, wt, *tables())
    lane = pl.BlockSpec((TOK, CH // 2), lambda c: (0, c))
    out, gq, gk, gv, gf = pl.pallas_call(
        finish,
        grid=(2,),
        out_shape=(flat, flat, flat, flat, jax.ShapeDtypeStruct((2, TOK, CH), F32)),
        in_specs=[
            lane,
            lane,
            pl.BlockSpec((NS // 2, 2, OWN, TOK), lambda c: (c, 0, 0, 0)),
            pl.BlockSpec((NS // 2, OWN, TOK), lambda c: (c, 0, 0)),
            lane,
            lane,
        ],
        out_specs=(lane, lane, lane, lane, pl.BlockSpec((2, TOK, CH // 2), lambda c: (0, 0, c))),
        compiler_params=pltpu.CompilerParams(vmem_limit_bytes=56 * 1024 * 1024),
    )(out, gq, gfr, gmr, keys, values)
    return out, gq, gk, gv, gf.reshape(2, 1, TOK, CH)


def solution(mesh):
    io = P("seq", "tp")
    spectrum = P(None, "seq", None, "tp")
    return jax.shard_map(
        shards,
        mesh=mesh,
        in_specs=(io, io, io, spectrum, P("tp", "seq"), io),
        out_specs=(io, io, io, io, spectrum),
        check_vma=False,
    )
```
